128 devices in a mesh: gx: 16 (over y, x_hi, core), gy: 8 (over x_lo, z).
Axes of the slice: x: 4 (x_hi: 2, x_lo: 2; x = x_hi * 2 + x_lo), y: 4, z: 4, core: 2. Of those that a mesh axis runs over, the one named last changes fastest.
Arguments:
- particle_count: int32 [8, 1024, 2048], P(None, ('gx', 'gy')), may hold values from 0 to 12
- drag_coeff: float32 [8, 1024, 2048], P(None, ('gx', 'gy')), may hold values from 0.05 to 2
- particle_velocity: float32 [3, 8, 1024, 2048], P(None, None, ('gx', 'gy')), may hold values from -6 to 6
- fluid_velocity: float32 [3, 8, 1024, 2048], P(None, None, 'gy', 'gx'), may hold values from -6 to 6
Outputs:
- pressure: float32 [8, 1024, 2048], P(None, 'gy', 'gx')
- new_velocity: float32 [3, 8, 1024, 2048], P(None, None, ('gx', 'gy'))
- pressure_gradient: float32 [3, 8, 1024, 2048], P(None, None, ('gx', 'gy'))
The draws below stay inside these ranges and needn't reach their ends.
All inputs are finite; a program needn't handle non-finite values.
Results may differ from the reference program's by a relative error of at most 0.00002.
Values sent between devices are 32-bit elements; how exact they have to be, the bound alone decides.
No kernel may reach another device: no remote copies, remote signals or barrier semaphores. Data moves between devices by JAX's collectives and lax.ppermute only.
A program may use at most 64 MiB of HBM per device.

```python
import math
import jax
import jax.numpy as jnp

NZ = 8
SWEEPS = 8
NX = 1024
NY = 2048


def place_ends(result, rng, least, top_value):
    extent = result.shape
    spot = [jax.random.randint(jax.random.fold_in(rng, axis), (), 0, extent[axis]) for axis in range(len(extent))]
    result = result.at[tuple(spot)].set(least)
    longest = extent.index(max(extent))
    spot[longest] = (spot[longest] + 1) % extent[longest]
    return result.at[tuple(spot)].set(top_value)


def levels(own_key, dims, shards, low, high):
    def one(axis_at, blocks):
        steps = jax.random.uniform(jax.random.fold_in(jax.random.fold_in(own_key, 6), axis_at), (blocks,), jnp.float32, low / len(shards), high / len(shards))
        return jnp.repeat(jnp.exp(steps), dims[axis_at] // blocks).reshape((-1,) + (1,) * (len(dims) - axis_at - 1))

    gain = one(*shards[0])
    for cut in shards[1:]:
        gain = gain * one(*cut)
    return gain


def gaussian(key, dims, width, reach, split=(), held_as=jnp.bfloat16):
    level = levels(key, dims, split, -0.22, 0.18) if split else 1.0
    entries = jax.random.normal(key, dims, jnp.float32) * width * level
    return jnp.minimum(jnp.maximum(entries, -reach), reach).astype(held_as)


def setup_inputs(seed: int = 0) -> dict:
    arg_keys = jax.random.split(jax.random.key(seed), 5)
    particle_count = place_ends(jax.random.randint(arg_keys[0], (NZ, NX, NY), 0, 13), jax.random.fold_in(arg_keys[0], 1), 0, 12).astype(jnp.int32)
    drag_coeff = jnp.clip(jnp.exp(math.log(2.0) - 3.6888794 * jax.random.uniform(arg_keys[1], (NZ, NX, NY), jnp.float32) ** levels(arg_keys[1], (NZ, NX, NY), ((1, 128),), -0.2, 0.2)), 0.05, 2.0)
    particle_velocity = gaussian(arg_keys[2], (3, NZ, NX, NY), 1.0, 6.0, ((2, 128),), jnp.float32)
    fluid_velocity = gaussian(arg_keys[3], (3, NZ, NX, NY), 1.0, 6.0, ((2, 8), (3, 16)), jnp.float32)
    return {"particle_count": particle_count, "drag_coeff": drag_coeff, "particle_velocity": particle_velocity, "fluid_velocity": fluid_velocity}


particle_volume = 0.05
time_step = 0.5
viscosity = 0.1


def pad_depth(values):
    widths = [(0, 0)] * (values.ndim - 3) + [(1, 1), (0, 0), (0, 0)]
    return jnp.pad(values, widths)


def pad_plane(values):
    widths = [(0, 0)] * (values.ndim - 2) + [(1, 1), (1, 1)]
    return jnp.pad(values, widths)


def middle(values):
    return values[..., 1:-1, 1:-1, 1:-1]


def neighbour(values, which):
    if which == 0:
        return values[..., 2:, 1:-1, 1:-1]
    if which == 1:
        return values[..., :-2, 1:-1, 1:-1]
    if which == 2:
        return values[..., 1:-1, 2:, 1:-1]
    if which == 3:
        return values[..., 1:-1, :-2, 1:-1]
    if which == 4:
        return values[..., 1:-1, 1:-1, 2:]
    return values[..., 1:-1, 1:-1, :-2]


def face_weights(voids_wide):
    padded = pad_depth(voids_wide)
    centre = middle(padded)
    weights = jnp.stack([0.5 * (centre + neighbour(padded, which)) for which in range(6)])
    weight_sum = weights[0]
    for which in range(1, 6):
        weight_sum = weight_sum + weights[which]
    return weights, weight_sum


def momentum(velocity_wide, weights, voids, drag, drag_force):
    padded = pad_depth(velocity_wide)
    centre = middle(padded)
    diffusion = jnp.zeros_like(centre)
    for which in range(6):
        diffusion = diffusion + weights[which][None] * (neighbour(padded, which) - centre)
    return (voids[None] * centre + time_step * viscosity * diffusion + time_step * drag_force) / (voids[None] + time_step * drag[None])


def divergence(flux_wide):
    first = flux_wide[0][:, 2:, 1:-1] - flux_wide[0][:, :-2, 1:-1]
    second = flux_wide[1][:, 1:-1, 2:] - flux_wide[1][:, 1:-1, :-2]
    normal = pad_depth(flux_wide[2])[:, 1:-1, 1:-1]
    third = normal[2:] - normal[:-2]
    return 0.5 * (first + second + third) / time_step


def jacobi_sweep(pressure_wide, weights, weight_sum, source):
    padded = pad_depth(pressure_wide)
    total = weights[0] * neighbour(padded, 0)
    for which in range(1, 6):
        total = total + weights[which] * neighbour(padded, which)
    return (total - source) / weight_sum


def gradient_of(pressure_wide):
    padded = pad_depth(pressure_wide)
    first = 0.5 * (padded[1:-1, 2:, 1:-1] - padded[1:-1, :-2, 1:-1])
    second = 0.5 * (padded[1:-1, 1:-1, 2:] - padded[1:-1, 1:-1, :-2])
    third = 0.5 * (padded[2:, 1:-1, 1:-1] - padded[:-2, 1:-1, 1:-1])
    return jnp.stack([first, second, third])


def reference(particle_count, drag_coeff, particle_velocity, fluid_velocity):
    voids = 1.0 - particle_count.astype(jnp.float32) * particle_volume
    drag_force = drag_coeff[None] * particle_velocity
    weights, weight_sum = face_weights(pad_plane(voids))
    predicted = momentum(pad_plane(fluid_velocity), weights, voids, drag_coeff, drag_force)
    flux = voids[None] * predicted
    source = divergence(pad_plane(flux))
    pressure = (-source) / weight_sum
    for sweep_index in range(SWEEPS - 1):
        pressure = jacobi_sweep(pad_plane(pressure), weights, weight_sum, source)
    slopes = gradient_of(pad_plane(pressure))
    velocity = predicted - time_step * slopes
    return pressure, velocity, slopes
```

```python
import functools

import jax
import jax.numpy as jnp
from jax import lax
from jax.experimental import pallas as pl
from jax.experimental.pallas import tpu as pltpu
from jax.sharding import PartitionSpec as P

SWEEPS = 8

particle_volume = 0.05
time_step = 0.5
viscosity = 0.1

ROWS = 8
PLANES = 8
GROUPS = 16
LANES = 128
TILE = (PLANES, LANES)
WIDE = 3 * ROWS
AXES = ("gx", "gy")
f32 = jnp.float32


def place():
    return lax.axis_index("gx") * lax.axis_size("gy") + lax.axis_index("gy")


def lane_ids():
    return lax.broadcasted_iota(jnp.int32, TILE, 1)


def plane_ids():
    return lax.broadcasted_iota(jnp.int32, TILE, 0)


def plane_up(tile):
    return pltpu.roll(tile, PLANES - 1, 0)


def plane_down(tile):
    return pltpu.roll(tile, 1, 0)


def column_neighbours(tiles):
    lanes = lane_ids()
    last, first = lanes == LANES - 1, lanes == 0
    ahead = [pltpu.roll(tile, LANES - 1, 1) for tile in tiles]
    behind = [pltpu.roll(tile, 1, 1) for tile in tiles]
    n = len(tiles)
    up = [jnp.where(last, ahead[g + 1], ahead[g]) if g < n - 1 else ahead[g] for g in range(n)]
    down = [jnp.where(first, behind[g - 1], behind[g]) if g > 0 else behind[g] for g in range(n)]
    return up, down


def no_column_up(g, tile):
    return jnp.where(lane_ids() == LANES - 1, 0.0, tile) if g == GROUPS - 1 else tile


def no_column_down(g, tile):
    return jnp.where(lane_ids() == 0, 0.0, tile) if g == 0 else tile


def weighted_sum(weights, row, g, tile, up, down, row_up, row_down):
    total = weights[row, 0, g] * plane_up(tile) + weights[row, 1, g] * plane_down(tile)
    total = total + (weights[row, 2, g] * row_up + weights[row, 3, g] * row_down)
    return total + (weights[row, 4, g] * up + weights[row, 5, g] * down)


def particle_kernel(count, drag, velocity, voids, drag_out, force, first_message, second_message):
    even = lax.rem(lax.axis_index("gy"), 2) == 0
    first_row = jnp.where(even, ROWS - 1, 0)
    second_row = ROWS - 1 - first_row
    for g in range(GROUPS):
        columns = pl.ds(g * LANES, LANES)
        void = jnp.swapaxes(1.0 - count[:, :, columns].astype(f32) * particle_volume, 0, 1)
        voids[:, g] = void
        first_message[0:ROWS, g] = void
        second_message[0:ROWS, g] = void
        drags = drag[:, :, columns]
        drag_out[:, g] = jnp.swapaxes(drags, 0, 1)
        for k in range(3):
            force[k, :, g] = jnp.swapaxes(time_step * drags * velocity[k, :, :, columns], 0, 1)
    for message, row in ((first_message, first_row), (second_message, second_row)):
        message[ROWS] = drag_out[row]
        message[ROWS + 1] = force[0, row]


def coefficient_kernel(
    voids, drag, force, first, second, weights, inverse_sum, centre, spread, given, voids_near, voids_wide
):
    device = place()
    even = lax.rem(lax.axis_index("gy"), 2) == 0
    devices = lax.axis_size("gx") * lax.axis_size("gy")
    low_there = (device > 0).astype(f32)
    high_there = (device < devices - 1).astype(f32)
    first_at = jnp.where(even, 2 * ROWS, 0)
    second_at = 2 * ROWS - first_at
    first_there = jnp.where(even, high_there, low_there)
    second_there = jnp.where(even, low_there, high_there)

    @pl.loop(0, ROWS)
    def _(row):
        voids_wide[first_at + row] = first[row] * first_there
        voids_wide[second_at + row] = second[row] * second_there
        voids_wide[ROWS + row] = voids[row]

    planes = plane_ids()

    def row_weights(row):
        tiles = [voids_wide[row, g] for g in range(GROUPS)]
        ups, downs = column_neighbours(tiles)
        for g in range(GROUPS):
            tile = tiles[g]
            near = [
                jnp.where(planes == PLANES - 1, 0.0, plane_up(tile)),
                jnp.where(planes == 0, 0.0, plane_down(tile)),
                voids_wide[row + 1, g],
                voids_wide[row - 1, g],
                no_column_up(g, ups[g]),
                no_column_down(g, downs[g]),
            ]
            faces = [0.5 * (tile + other) for other in near]
            total = faces[0]
            for face in faces[1:]:
                total = total + face
            inverse = jnp.where(tile > 0.0, 1.0 / total, 0.0)
            scaled = [face * inverse for face in faces]
            scaled[0] = jnp.where(planes == PLANES - 1, 0.0, scaled[0])
            scaled[1] = jnp.where(planes == 0, 0.0, scaled[1])
            scaled[4] = no_column_up(g, scaled[4])
            scaled[5] = no_column_down(g, scaled[5])
            for n in range(6):
                weights[row - 1, n, g] = scaled[n]
            yield g, tile, total, inverse

    @pl.loop(1, ROWS - 1)
    def _(row):
        for _ in row_weights(row):
            pass

    @pl.loop(2 * ROWS + 1, WIDE - 1)
    def _(row):
        for _ in row_weights(row):
            pass

    def momentum_row(row, drag_at, force_at):
        for g, tile, total, inverse in row_weights(row):
            scale = 1.0 / (tile + time_step * drag_at(g))
            near = row - (ROWS - 1)
            voids_near[near, g] = tile
            centre[near, g] = (tile - time_step * viscosity * total) * scale
            spread[near, g] = (time_step * viscosity * total) * scale
            for k, value in enumerate(force_at(g)):
                given[k, near, g] = value * scale
            yield g, inverse

    @pl.loop(0, ROWS)
    def _(row):
        for g, inverse in momentum_row(
            row + ROWS, lambda g: drag[row, g], lambda g: [force[k, row, g] for k in range(3)]
        ):
            inverse_sum[row, g] = inverse

    for message, at in ((first, first_at), (second, second_at)):
        row = jnp.where(at == 0, ROWS - 1, 2 * ROWS)
        for _ in momentum_row(row, lambda g: message[ROWS, g], lambda g: [message[ROWS + 1, g]]):
            pass


def edge_kernel(velocity, first, second):
    even = lax.rem(lax.axis_index("gy"), 2) == 0
    first_row = jnp.where(even, ROWS - 2, 0)
    for message, pair, single in (
        (first, first_row, jnp.where(even, ROWS - 1, 0)),
        (second, ROWS - 2 - first_row, jnp.where(even, 0, ROWS - 1)),
    ):
        for g in range(GROUPS):
            message[0, g] = velocity[g, 0, pair]
            message[1, g] = velocity[g, 0, pair + 1]
            message[2, g] = velocity[g, 1, single]
            message[3, g] = velocity[g, 2, single]


def momentum_kernel(
    velocity, first, second, weights, inverse_sum, centre, spread, given, voids_near, predicted, source, wide, flux
):
    device = place()
    even = lax.rem(lax.axis_index("gy"), 2) == 0
    devices = lax.axis_size("gx") * lax.axis_size("gy")
    low_there = (device > 0).astype(f32)
    high_there = (device < devices - 1).astype(f32)
    for message, is_high in ((first, even), (second, jnp.logical_not(even))):
        there = jnp.where(is_high, high_there, low_there)
        pair = jnp.where(is_high, ROWS + 2, 0)
        single = jnp.where(is_high, ROWS + 2, 1)
        for g in range(GROUPS):
            wide[0, pair, g] = message[0, g] * there
            wide[0, pair + 1, g] = message[1, g] * there
            wide[1, single, g] = message[2, g] * there
            wide[2, single, g] = message[3, g] * there

    @pl.loop(0, ROWS)
    def _(row):
        for g in range(GROUPS):
            for k in range(3):
                wide[k, row + 2, g] = velocity[g, k, row]

    planes = plane_ids()

    def predict(k, near):
        tiles = [wide[k, near + 1, g] for g in range(GROUPS)]
        ups, downs = column_neighbours(tiles)
        for g in range(GROUPS):
            around = weighted_sum(
                weights, near + (ROWS - 2), g, tiles[g], ups[g], downs[g], wide[k, near + 2, g], wide[k, near, g]
            )
            yield centre[near, g] * tiles[g] + spread[near, g] * around + given[k, near, g]

    @pl.loop(0, ROWS + 2)
    def _(near):
        for g, value in enumerate(predict(0, near)):
            flux[near, g] = voids_near[near, g] * value
            wide[0, near, g] = value

    @pl.loop(0, ROWS)
    def _(row):
        near = row + 1
        second_flux = []
        for g, value in enumerate(predict(1, near)):
            predicted[1, row, g] = value
            second_flux.append(voids_near[near, g] * value)
        ups, downs = column_neighbours(second_flux)
        for g, value in enumerate(predict(2, near)):
            predicted[2, row, g] = value
            predicted[0, row, g] = wide[0, near, g]
            third_flux = voids_near[near, g] * value
            change = flux[near + 1, g] - flux[near - 1, g]
            change = change + (no_column_up(g, ups[g]) - no_column_down(g, downs[g]))
            change = change + (
                jnp.where(planes == PLANES - 1, 0.0, plane_up(third_flux))
                - jnp.where(planes == 0, 0.0, plane_down(third_flux))
            )
            source[row, g] = change * inverse_sum[row, g]


def sweep_kernel(source, first, second, weights, pressure, near_pressure, source_wide, one, other):
    device = place()
    even = lax.rem(lax.axis_index("gy"), 2) == 0
    devices = lax.axis_size("gx") * lax.axis_size("gy")
    low_there = (device > 0).astype(f32)
    high_there = (device < devices - 1).astype(f32)
    first_at = jnp.where(even, 2 * ROWS, 0)
    second_at = 2 * ROWS - first_at
    first_there = jnp.where(even, high_there, low_there)
    second_there = jnp.where(even, low_there, high_there)

    @pl.loop(0, ROWS)
    def _(row):
        for at, value in (
            (first_at + row, first[row] * first_there),
            (second_at + row, second[row] * second_there),
            (ROWS + row, source[row]),
        ):
            source_wide[at] = value
            one[at] = -value

    now, later = one, other
    for sweep in range(1, SWEEPS):

        def sweep_row(row, now=now, later=later):
            tiles = [now[row, g] for g in range(GROUPS)]
            ups, downs = column_neighbours(tiles)
            for g in range(GROUPS):
                around = weighted_sum(
                    weights, row - 1, g, tiles[g], ups[g], downs[g], now[row + 1, g], now[row - 1, g]
                )
                later[row, g] = around - source_wide[row, g]

        pl.loop(sweep, WIDE - sweep)(sweep_row)
        now, later = later, now

    @pl.loop(0, ROWS)
    def _(row):
        for g in range(GROUPS):
            pressure[g, row] = now[row + ROWS, g]

    @pl.loop(0, ROWS + 2)
    def _(row):
        near_pressure[row] = now[row + ROWS - 1]


def correct_kernel(near_pressure, predicted, velocity, slopes):
    planes = plane_ids()
    held = [[[None] * ROWS for _ in range(GROUPS)] for _ in range(3)]
    for row in range(ROWS):
        tiles = [near_pressure[row + 1, g] for g in range(GROUPS)]
        ups, downs = column_neighbours(tiles)
        for g in range(GROUPS):
            tile = tiles[g]
            held[0][g][row] = 0.5 * (near_pressure[row + 2, g] - near_pressure[row, g])
            held[1][g][row] = 0.5 * (no_column_up(g, ups[g]) - no_column_down(g, downs[g]))
            held[2][g][row] = 0.5 * (
                jnp.where(planes == PLANES - 1, 0.0, plane_up(tile)) - jnp.where(planes == 0, 0.0, plane_down(tile))
            )
    for g in range(GROUPS):
        columns = pl.ds(g * LANES, LANES)
        for k in range(3):
            slope = jnp.stack(held[k][g])
            slopes[k, :, :, columns] = jnp.swapaxes(slope, 0, 1)
            velocity[k, :, :, columns] = jnp.swapaxes(predicted[k, :, g] - time_step * slope, 0, 1)


def call(kernel, args, outs, scratch=(), flops=0):
    vmem = pl.BlockSpec(memory_space=pltpu.VMEM)
    shapes = [jax.ShapeDtypeStruct(shape, f32) for shape in outs]
    moved = sum(arg.size for arg in args) * 4 + sum(shape.size for shape in shapes) * 4
    return pl.pallas_call(
        kernel,
        out_shape=shapes,
        in_specs=[vmem] * len(args),
        out_specs=[vmem] * len(outs),
        scratch_shapes=[pltpu.VMEM(shape, f32) for shape in scratch],
        cost_estimate=pl.CostEstimate(flops=flops, bytes_accessed=moved, transcendentals=0),
        compiler_params=pltpu.CompilerParams(vmem_limit_bytes=40 * 1024 * 1024),
        name=kernel.__name__,
    )(*args)


def swap(first, second):
    devices = lax.axis_size("gx") * lax.axis_size("gy")
    inner = [(d, d ^ 1) for d in range(devices)]
    outer = [(d, (((d + 1) % devices) ^ 1) - 1) for d in range(devices)]
    outer = [(a, b % devices) for a, b in outer]
    return lax.ppermute(first, AXES, inner), lax.ppermute(second, AXES, outer)


def shards(particle_count, drag_coeff, particle_velocity, fluid_velocity):
    along, across = lax.axis_size("gy"), lax.axis_size("gx")
    field = (GROUPS, PLANES, LANES)
    own = (ROWS,) + field
    near = (ROWS + 2,) + field

    voids, drag, force, first, second = call(
        particle_kernel,
        (particle_count, drag_coeff, particle_velocity),
        [own, own, (3,) + own, near, near],
    )

    blocks = fluid_velocity.reshape(3, PLANES, across // along, along, ROWS, LANES)
    blocks = blocks.transpose(3, 2, 0, 4, 1, 5)
    blocks = lax.all_to_all(blocks, "gy", split_axis=0, concat_axis=0, tiled=True)
    blocks = blocks.reshape(across, 3, ROWS, PLANES, LANES)
    blocks, first, second = lax.optimization_barrier((blocks, first, second))
    first, second = swap(first, second)
    slab = lax.all_to_all(blocks, "gx", split_axis=0, concat_axis=0, tiled=True)

    weights, inverse_sum, centre, spread, given, voids_near = call(
        coefficient_kernel,
        (voids, drag, force, first, second),
        [(WIDE - 2, 6) + field, own, near, near, (3,) + near, near],
        [(WIDE,) + field],
    )

    edges = call(edge_kernel, (slab,), [(4,) + field] * 2)
    first, second = swap(*edges)
    predicted, source = call(
        momentum_kernel,
        (slab, first, second, weights, inverse_sum, centre, spread, given, voids_near),
        [(3,) + own, own],
        [(3, ROWS + 4) + field, near],
    )
    first, second = swap(source, source)
    pressure, near_pressure = call(
        sweep_kernel,
        (source, first, second, weights),
        [(GROUPS, ROWS, PLANES, LANES), near],
        [(WIDE,) + field] * 3,
    )

    velocity, slopes = call(
        correct_kernel, (near_pressure, predicted), [(3, PLANES, ROWS, GROUPS * LANES)] * 2
    )

    pressure = lax.all_to_all(pressure, "gx", split_axis=0, concat_axis=0, tiled=True)
    pressure = lax.all_to_all(pressure, "gy", split_axis=0, concat_axis=0, tiled=True)
    pressure = pressure.reshape(along, across // along, ROWS, PLANES, LANES)
    pressure = pressure.transpose(3, 1, 0, 2, 4).reshape(PLANES, across * ROWS, LANES)
    return (pressure, velocity, slopes)


def solution(mesh):
    placed = (
        P(None, ("gx", "gy"), None),
        P(None, ("gx", "gy"), None),
        P(None, None, ("gx", "gy"), None),
        P(None, None, "gy", "gx"),
    )
    return jax.shard_map(
        shards,
        mesh=mesh,
        in_specs=placed,
        out_specs=(
            P(None, "gy", "gx"),
            P(None, None, ("gx", "gy"), None),
            P(None, None, ("gx", "gy"), None),
        ),
        check_vma=False,
    )
```

```python
import functools

import jax
import jax.numpy as jnp
from jax import lax
from jax.experimental import pallas as pl
from jax.experimental.pallas import tpu as pltpu
from jax.sharding import PartitionSpec as P

SWEEPS = 8

particle_volume = 0.05
time_step = 0.5
viscosity = 0.1

ROWS = 8
PLANES = 8
GROUPS = 16
LANES = 128
TILE = (PLANES, LANES)
WIDE = 3 * ROWS
AXES = ("gx", "gy")
f32 = jnp.float32


def place():
    return lax.axis_index("gx") * lax.axis_size("gy") + lax.axis_index("gy")


def lane_ids():
    return lax.broadcasted_iota(jnp.int32, TILE, 1)


def plane_ids():
    return lax.broadcasted_iota(jnp.int32, TILE, 0)


def plane_up(tile):
    return pltpu.roll(tile, PLANES - 1, 0)


def plane_down(tile):
    return pltpu.roll(tile, 1, 0)


def column_neighbours(tiles):
    lanes = lane_ids()
    last, first = lanes == LANES - 1, lanes == 0
    ahead = [pltpu.roll(tile, LANES - 1, 1) for tile in tiles]
    behind = [pltpu.roll(tile, 1, 1) for tile in tiles]
    n = len(tiles)
    up = [jnp.where(last, ahead[g + 1], ahead[g]) if g < n - 1 else ahead[g] for g in range(n)]
    down = [jnp.where(first, behind[g - 1], behind[g]) if g > 0 else behind[g] for g in range(n)]
    return up, down


def no_column_up(g, tile):
    return jnp.where(lane_ids() == LANES - 1, 0.0, tile) if g == GROUPS - 1 else tile


def no_column_down(g, tile):
    return jnp.where(lane_ids() == 0, 0.0, tile) if g == 0 else tile


def weighted_sum(weights, row, g, tile, up, down, row_up, row_down):
    total = weights[row, 0, g] * plane_up(tile) + weights[row, 1, g] * plane_down(tile)
    total = total + (weights[row, 2, g] * row_up + weights[row, 3, g] * row_down)
    return total + (weights[row, 4, g] * up + weights[row, 5, g] * down)


def block_kernel(velocity, blocks, staged, arrived):
    copies = []
    for k in range(3):
        for z in range(0, PLANES, 2):
            planes = pl.ds(z, 2)
            copy = pltpu.make_async_copy(
                velocity.at[k, planes], staged.at[k, planes], arrived.at[k * (PLANES // 2) + z // 2]
            )
            copy.start()
            copies.append(copy)
    along, groups = blocks.shape[:2]
    for k in range(3):
        for copy in copies[k * (PLANES // 2) : (k + 1) * (PLANES // 2)]:
            copy.wait()
        for chunk in range(along * groups):
            rows = staged[k, :, pl.ds(chunk * ROWS, ROWS), :]
            blocks[chunk % along, chunk // along, k] = jnp.swapaxes(rows, 0, 1)


def particle_kernel(count, drag, velocity, voids, drag_out, force, first_near, second_near, first_far, second_far):
    even = lax.rem(lax.axis_index("gy"), 2) == 0
    for g in range(GROUPS):
        columns = pl.ds(g * LANES, LANES)
        voids[:, g] = jnp.swapaxes(1.0 - count[:, :, columns].astype(f32) * particle_volume, 0, 1)
        drags = drag[:, :, columns]
        drag_out[:, g] = jnp.swapaxes(drags, 0, 1)
        for k in range(3):
            force[k, :, g] = jnp.swapaxes(time_step * drags * velocity[k, :, :, columns], 0, 1)
    for near, far, last in ((first_near, first_far, even), (second_near, second_far, jnp.logical_not(even))):
        pair = jnp.where(last, ROWS - 2, 0)
        single = jnp.where(last, ROWS - 1, 0)
        rest = jnp.where(last, 0, 2)
        near[0:2] = voids[pl.ds(pair, 2)]
        near[2] = drag_out[single]
        near[3] = force[0, single]
        far[...] = voids[pl.ds(rest, ROWS - 2)]


class Side:
    def __init__(self, first):
        even = lax.rem(lax.axis_index("gy"), 2) == 0
        self.high = even if first else jnp.logical_not(even)
        devices = lax.axis_size("gx") * lax.axis_size("gy")
        low_there = (place() > 0).astype(f32)
        high_there = (place() < devices - 1).astype(f32)
        self.there = jnp.where(self.high, high_there, low_there)

    def at(self, high, low):
        return jnp.where(self.high, high, low)


def face_row(voids, row, store):
    planes = plane_ids()
    tiles = [voids[row, g] for g in range(GROUPS)]
    ups, downs = column_neighbours(tiles)
    for g in range(GROUPS):
        tile = tiles[g]
        near = [
            jnp.where(planes == PLANES - 1, 0.0, plane_up(tile)),
            jnp.where(planes == 0, 0.0, plane_down(tile)),
            voids[row + 1, g],
            voids[row - 1, g],
            no_column_up(g, ups[g]),
            no_column_down(g, downs[g]),
        ]
        faces = [0.5 * (tile + other) for other in near]
        total = faces[0]
        for face in faces[1:]:
            total = total + face
        inverse = jnp.where(tile > 0.0, 1.0 / total, 0.0)
        scaled = [face * inverse for face in faces]
        scaled[0] = jnp.where(planes == PLANES - 1, 0.0, scaled[0])
        scaled[1] = jnp.where(planes == 0, 0.0, scaled[1])
        scaled[4] = no_column_up(g, scaled[4])
        scaled[5] = no_column_down(g, scaled[5])
        store(g, scaled, tile, total, inverse)


def coefficient_kernel(voids, drag, force, first, second, weights, inverse_sum, centre, spread, given, voids_near):
    for message, side in ((first, Side(True)), (second, Side(False))):
        at = side.at(ROWS + 2, 0)
        for n in range(2):
            voids_near[at + n] = message[n] * side.there

    @pl.loop(0, ROWS)
    def _(row):
        voids_near[row + 2] = voids[row]

    def momentum_row(near, drag_at, force_at, own=None):
        def store(g, scaled, void, total, inverse):
            for n in range(6):
                weights[near, n, g] = scaled[n]
            scale = 1.0 / (void + time_step * drag_at(g))
            centre[near, g] = (void - time_step * viscosity * total) * scale
            spread[near, g] = (time_step * viscosity * total) * scale
            for k, value in enumerate(force_at(g)):
                given[k, near, g] = value * scale
            if own is not None:
                inverse_sum[own, g] = inverse

        face_row(voids_near, near + 1, store)

    @pl.loop(0, ROWS, step=2)
    def _(start):
        for row in (start, start + 1):
            momentum_row(
                row + 1,
                lambda g, row=row: drag[row, g],
                lambda g, row=row: [force[k, row, g] for k in range(3)],
                row,
            )

    for message, side in ((first, Side(True)), (second, Side(False))):
        momentum_row(
            side.at(ROWS + 1, 0), lambda g, m=message: m[2, g], lambda g, m=message: [m[3, g]]
        )


def outer_kernel(voids_near, first, second, near_weights, weights, wide):
    for message, side in ((first, Side(True)), (second, Side(False))):
        at = side.at(2 * ROWS + 2, 0)
        for n in range(ROWS - 2):
            wide[at + n] = message[n] * side.there

    @pl.loop(0, ROWS + 4)
    def _(row):
        wide[row + ROWS - 2] = voids_near[row]

    @pl.loop(0, ROWS + 2)
    def _(row):
        weights[row + ROWS - 2] = near_weights[row]

    def outer_row(row):
        def store(g, scaled, void, total, inverse):
            for n in range(6):
                weights[row - 1, n, g] = scaled[n]

        face_row(wide, row, store)

    @pl.loop(1, ROWS - 1, step=2)
    def _(start):
        for row in (start, start + 1, start + 2 * ROWS, start + 2 * ROWS + 1):
            outer_row(row)


def edge_kernel(velocity, first, second):
    even = lax.rem(lax.axis_index("gy"), 2) == 0
    first_row = jnp.where(even, ROWS - 2, 0)
    for message, pair, single in (
        (first, first_row, jnp.where(even, ROWS - 1, 0)),
        (second, ROWS - 2 - first_row, jnp.where(even, 0, ROWS - 1)),
    ):
        for g in range(GROUPS):
            message[0, g] = velocity[g, 0, pair]
            message[1, g] = velocity[g, 0, pair + 1]
            message[2, g] = velocity[g, 1, single]
            message[3, g] = velocity[g, 2, single]


def momentum_kernel(
    velocity, first, second, weights, inverse_sum, centre, spread, given, voids_near, predicted, source, wide, flux
):
    for message, side in ((first, Side(True)), (second, Side(False))):
        pair = side.at(ROWS + 2, 0)
        single = side.at(ROWS + 2, 1)
        for g in range(GROUPS):
            wide[0, pair, g] = message[0, g] * side.there
            wide[0, pair + 1, g] = message[1, g] * side.there
            wide[1, single, g] = message[2, g] * side.there
            wide[2, single, g] = message[3, g] * side.there

    @pl.loop(0, ROWS, step=2)
    def _(start):
        for row in (start, start + 1):
            for g in range(GROUPS):
                for k in range(3):
                    wide[k, row + 2, g] = velocity[g, k, row]

    planes = plane_ids()

    def predict(k, near):
        tiles = [wide[k, near + 1, g] for g in range(GROUPS)]
        ups, downs = column_neighbours(tiles)
        for g in range(GROUPS):
            around = weighted_sum(
                weights, near, g, tiles[g], ups[g], downs[g], wide[k, near + 2, g], wide[k, near, g]
            )
            yield centre[near, g] * tiles[g] + spread[near, g] * around + given[k, near, g]

    @pl.loop(0, ROWS + 2, step=5)
    def _(start):
        for near in range(5):
            for g, value in enumerate(predict(0, start + near)):
                flux[0, start + near, g] = value
                flux[1, start + near, g] = voids_near[start + near + 1, g] * value

    @pl.loop(0, ROWS, step=4)
    def _(start):
        for row in range(4):
            row = start + row
            near = row + 1
            second_flux = []
            for g, value in enumerate(predict(1, near)):
                predicted[1, row, g] = value
                second_flux.append(voids_near[near + 1, g] * value)
            ups, downs = column_neighbours(second_flux)
            for g, value in enumerate(predict(2, near)):
                predicted[2, row, g] = value
                predicted[0, row, g] = flux[0, near, g]
                third_flux = voids_near[near + 1, g] * value
                change = flux[1, near + 1, g] - flux[1, near - 1, g]
                change = change + (no_column_up(g, ups[g]) - no_column_down(g, downs[g]))
                change = change + (
                    jnp.where(planes == PLANES - 1, 0.0, plane_up(third_flux))
                    - jnp.where(planes == 0, 0.0, plane_down(third_flux))
                )
                source[row, g] = change * inverse_sum[row, g]


def sweep_kernel(source, first, second, weights, pressure, near_pressure, source_wide, one, other):
    sides = Side(True).at(2 * ROWS, 0), Side(False).at(2 * ROWS, 0)
    there = Side(True).there, Side(False).there

    @pl.loop(0, ROWS, step=2)
    def _(start):
        for row in (start, start + 1):
            for at, value in (
                (sides[0] + row, first[row] * there[0]),
                (sides[1] + row, second[row] * there[1]),
                (ROWS + row, source[row]),
            ):
                source_wide[at] = value
                one[at] = -value

    def sweep_row(row, now, store):
        tiles = [now[row, g] for g in range(GROUPS)]
        ups, downs = column_neighbours(tiles)
        for g in range(GROUPS):
            around = weighted_sum(weights, row - 1, g, tiles[g], ups[g], downs[g], now[row + 1, g], now[row - 1, g])
            store(row, g, around - source_wide[row, g])

    now, later = one, other
    for sweep in range(1, SWEEPS - 1):
        half = (WIDE - 2 * sweep) // 2

        def half_sweep(start, now=now, later=later, half=half):
            def store(row, g, value):
                later[row, g] = value

            for row in range(half):
                sweep_row(start + row, now, store)

        pl.loop(sweep, WIDE - sweep, step=half)(half_sweep)
        now, later = later, now

    def keep(row, g, value):
        near_pressure[row - (ROWS - 1), g] = value

    @pl.loop(0, ROWS, step=4)
    def _(start):
        def store(row, g, value):
            keep(row, g, value)
            pressure[g, row - ROWS] = value

        for row in range(4):
            sweep_row(ROWS + start + row, now, store)

    for row in (ROWS - 1, 2 * ROWS):
        sweep_row(row, now, keep)


def correct_kernel(near_pressure, predicted, velocity, slopes):
    planes = plane_ids()
    held = [[[None] * ROWS for _ in range(GROUPS)] for _ in range(3)]
    for row in range(ROWS):
        tiles = [near_pressure[row + 1, g] for g in range(GROUPS)]
        ups, downs = column_neighbours(tiles)
        for g in range(GROUPS):
            tile = tiles[g]
            held[0][g][row] = 0.5 * (near_pressure[row + 2, g] - near_pressure[row, g])
            held[1][g][row] = 0.5 * (no_column_up(g, ups[g]) - no_column_down(g, downs[g]))
            held[2][g][row] = 0.5 * (
                jnp.where(planes == PLANES - 1, 0.0, plane_up(tile)) - jnp.where(planes == 0, 0.0, plane_down(tile))
            )
    for g in range(GROUPS):
        columns = pl.ds(g * LANES, LANES)
        for k in range(3):
            slope = jnp.stack(held[k][g])
            slopes[k, :, :, columns] = jnp.swapaxes(slope, 0, 1)
            velocity[k, :, :, columns] = jnp.swapaxes(predicted[k, :, g] - time_step * slope, 0, 1)


def call(kernel, args, outs, scratch=(), vmem=16, spaces=None):
    spec = pl.BlockSpec(memory_space=pltpu.VMEM)
    shapes = [jax.ShapeDtypeStruct(shape, f32) for shape in outs]
    moved = sum(arg.size for arg in args) * 4 + sum(shape.size for shape in shapes) * 4
    return pl.pallas_call(
        kernel,
        out_shape=shapes,
        in_specs=spaces or [spec] * len(args),
        out_specs=[spec] * len(outs),
        scratch_shapes=[pltpu.VMEM(shape, f32) if isinstance(shape, tuple) else shape for shape in scratch],
        cost_estimate=pl.CostEstimate(flops=0, bytes_accessed=moved, transcendentals=0),
        compiler_params=pltpu.CompilerParams(vmem_limit_bytes=vmem * 1024 * 1024),
        name=kernel.__name__,
    )(*args)


def swap(first, second):
    devices = lax.axis_size("gx") * lax.axis_size("gy")
    inner = [(d, d ^ 1) for d in range(devices)]
    outer = [(d, (((d + 1) % devices) ^ 1) - 1) for d in range(devices)]
    outer = [(a, b % devices) for a, b in outer]
    return lax.ppermute(first, AXES, inner), lax.ppermute(second, AXES, outer)


def shards(particle_count, drag_coeff, particle_velocity, fluid_velocity):
    along, across = lax.axis_size("gy"), lax.axis_size("gx")
    field = (GROUPS, PLANES, LANES)
    own = (ROWS,) + field
    near = (ROWS + 2,) + field

    voids, drag, force, first, second, first_far, second_far = call(
        particle_kernel,
        (particle_count, drag_coeff, particle_velocity),
        [own, own, (3,) + own, (4,) + field, (4,) + field, (ROWS - 2,) + field, (ROWS - 2,) + field],
    )
    (blocks,) = call(
        block_kernel,
        (fluid_velocity,),
        [(along, across // along, 3, ROWS, PLANES, LANES)],
        [(3, PLANES, across * ROWS, LANES), pltpu.SemaphoreType.DMA((3 * PLANES // 2,))],
        spaces=[pl.BlockSpec(memory_space=pl.ANY)],
    )
    first, second = swap(first, second)
    blocks = lax.all_to_all(blocks, "gy", split_axis=0, concat_axis=0, tiled=True)
    blocks = blocks.reshape(across, 3, ROWS, PLANES, LANES)
    blocks, first_far, second_far = lax.optimization_barrier((blocks, first_far, second_far))
    first_far, second_far = swap(first_far, second_far)
    slab = lax.all_to_all(blocks, "gx", split_axis=0, concat_axis=0, tiled=True)
    near_weights, inverse_sum, centre, spread, given, voids_near = call(
        coefficient_kernel,
        (voids, drag, force, first, second),
        [(ROWS + 2, 6) + field, own, near, near, (3,) + near, (ROWS + 4,) + field],
    )

    edges = call(edge_kernel, (slab,), [(4,) + field] * 2)
    first, second = swap(*edges)
    predicted, source = call(
        momentum_kernel,
        (slab, first, second, near_weights, inverse_sum, centre, spread, given, voids_near),
        [(3,) + own, own],
        [(3, ROWS + 4) + field, (2,) + near],
    )
    *_, first_far, second_far = lax.optimization_barrier((*edges, first_far, second_far))
    (weights,) = call(
        outer_kernel,
        (voids_near, first_far, second_far, near_weights),
        [(WIDE - 2, 6) + field],
        [(WIDE,) + field],
    )
    first, second = swap(source, source)
    pressure, near_pressure = call(
        sweep_kernel,
        (source, first, second, weights),
        [(GROUPS, ROWS, PLANES, LANES), near],
        [(WIDE,) + field] * 3,
    )

    velocity, slopes = call(
        correct_kernel, (near_pressure, predicted), [(3, PLANES, ROWS, GROUPS * LANES)] * 2
    )

    pressure = lax.all_to_all(pressure, "gx", split_axis=0, concat_axis=0, tiled=True)
    pressure = lax.all_to_all(pressure, "gy", split_axis=0, concat_axis=0, tiled=True)
    pressure = pressure.reshape(along, across // along, ROWS, PLANES, LANES)
    pressure = pressure.transpose(3, 1, 0, 2, 4).reshape(PLANES, across * ROWS, LANES)
    return (pressure, velocity, slopes)


def solution(mesh):
    placed = (
        P(None, ("gx", "gy"), None),
        P(None, ("gx", "gy"), None),
        P(None, None, ("gx", "gy"), None),
        P(None, None, "gy", "gx"),
    )
    return jax.shard_map(
        shards,
        mesh=mesh,
        in_specs=placed,
        out_specs=(
            P(None, "gy", "gx"),
            P(None, None, ("gx", "gy"), None),
            P(None, None, ("gx", "gy"), None),
        ),
        check_vma=False,
    )
```

```python
import functools

import jax
import jax.numpy as jnp
from jax import lax
from jax.experimental import pallas as pl
from jax.experimental.pallas import tpu as pltpu
from jax.sharding import PartitionSpec as P

SWEEPS = 8

particle_volume = 0.05
time_step = 0.5
viscosity = 0.1

ROWS = 8
PLANES = 8
GROUPS = 16
LANES = 128
TILE = (PLANES, LANES)
WIDE = 3 * ROWS
COVER = 6_000_000_000
AXES = ("gx", "gy")
f32 = jnp.float32


def place():
    return lax.axis_index("gx") * lax.axis_size("gy") + lax.axis_index("gy")


def lane_ids():
    return lax.broadcasted_iota(jnp.int32, TILE, 1)


def plane_ids():
    return lax.broadcasted_iota(jnp.int32, TILE, 0)


def plane_up(tile):
    return pltpu.roll(tile, PLANES - 1, 0)


def plane_down(tile):
    return pltpu.roll(tile, 1, 0)


def column_neighbours(tiles):
    lanes = lane_ids()
    last, first = lanes == LANES - 1, lanes == 0
    ahead = [pltpu.roll(tile, LANES - 1, 1) for tile in tiles]
    behind = [pltpu.roll(tile, 1, 1) for tile in tiles]
    n = len(tiles)
    up = [jnp.where(last, ahead[g + 1], ahead[g]) if g < n - 1 else ahead[g] for g in range(n)]
    down = [jnp.where(first, behind[g - 1], behind[g]) if g > 0 else behind[g] for g in range(n)]
    return up, down


def no_column_up(g, tile):
    return jnp.where(lane_ids() == LANES - 1, 0.0, tile) if g == GROUPS - 1 else tile


def no_column_down(g, tile):
    return jnp.where(lane_ids() == 0, 0.0, tile) if g == 0 else tile


def weighted_sum(weights, row, g, tile, up, down, row_up, row_down):
    total = weights[row, 0, g] * plane_up(tile) + weights[row, 1, g] * plane_down(tile)
    total = total + (weights[row, 2, g] * row_up + weights[row, 3, g] * row_down)
    return total + (weights[row, 4, g] * up + weights[row, 5, g] * down)


def block_kernel(velocity, blocks, turned, left):
    along, groups = blocks.shape[:2]
    copies = []
    for k in range(3):
        for part in range(groups):
            for chunk in range(along):
                rows = velocity[k, :, pl.ds((part * along + chunk) * ROWS, ROWS), :]
                turned[chunk, part, k] = jnp.swapaxes(rows, 0, 1)
            copies.append(pltpu.make_async_copy(turned.at[:, part, k], blocks.at[:, part, k], left.at[k, part]))
            copies[-1].start()
    for copy in copies:
        copy.wait()


def particle_kernel(count, drag, velocity, voids, drag_out, force, first_near, second_near, first_far, second_far):
    even = lax.rem(lax.axis_index("gy"), 2) == 0
    for g in range(GROUPS):
        columns = pl.ds(g * LANES, LANES)
        voids[:, g] = jnp.swapaxes(1.0 - count[:, :, columns].astype(f32) * particle_volume, 0, 1)
        drags = drag[:, :, columns]
        drag_out[:, g] = jnp.swapaxes(drags, 0, 1)
        for k in range(3):
            force[k, :, g] = jnp.swapaxes(time_step * drags * velocity[k, :, :, columns], 0, 1)
    for near, far, last in ((first_near, first_far, even), (second_near, second_far, jnp.logical_not(even))):
        pair = jnp.where(last, ROWS - 2, 0)
        single = jnp.where(last, ROWS - 1, 0)
        rest = jnp.where(last, 0, 2)
        near[0:2] = voids[pl.ds(pair, 2)]
        near[2] = drag_out[single]
        near[3] = force[0, single]
        far[...] = voids[pl.ds(rest, ROWS - 2)]


class Side:
    def __init__(self, first):
        even = lax.rem(lax.axis_index("gy"), 2) == 0
        self.high = even if first else jnp.logical_not(even)
        devices = lax.axis_size("gx") * lax.axis_size("gy")
        low_there = (place() > 0).astype(f32)
        high_there = (place() < devices - 1).astype(f32)
        self.there = jnp.where(self.high, high_there, low_there)

    def at(self, high, low):
        return jnp.where(self.high, high, low)


def face_row(voids, row, store):
    planes = plane_ids()
    tiles = [voids[row, g] for g in range(GROUPS)]
    ups, downs = column_neighbours(tiles)
    for g in range(GROUPS):
        tile = tiles[g]
        near = [
            jnp.where(planes == PLANES - 1, 0.0, plane_up(tile)),
            jnp.where(planes == 0, 0.0, plane_down(tile)),
            voids[row + 1, g],
            voids[row - 1, g],
            no_column_up(g, ups[g]),
            no_column_down(g, downs[g]),
        ]
        faces = [0.5 * (tile + other) for other in near]
        total = faces[0]
        for face in faces[1:]:
            total = total + face
        inverse = jnp.where(tile > 0.0, 1.0 / total, 0.0)
        scaled = [face * inverse for face in faces]
        scaled[0] = jnp.where(planes == PLANES - 1, 0.0, scaled[0])
        scaled[1] = jnp.where(planes == 0, 0.0, scaled[1])
        scaled[4] = no_column_up(g, scaled[4])
        scaled[5] = no_column_down(g, scaled[5])
        store(g, scaled, tile, total, inverse)


def coefficient_kernel(voids, drag, force, first, second, weights, inverse_sum, centre, spread, given, voids_near):
    for message, side in ((first, Side(True)), (second, Side(False))):
        at = side.at(ROWS + 2, 0)
        for n in range(2):
            voids_near[at + n] = message[n] * side.there

    @pl.loop(0, ROWS)
    def _(row):
        voids_near[row + 2] = voids[row]

    def momentum_row(near, drag_at, force_at, own=None):
        def store(g, scaled, void, total, inverse):
            for n in range(6):
                weights[near, n, g] = scaled[n]
            scale = 1.0 / (void + time_step * drag_at(g))
            centre[near, g] = (void - time_step * viscosity * total) * scale
            spread[near, g] = (time_step * viscosity * total) * scale
            for k, value in enumerate(force_at(g)):
                given[k, near, g] = value * scale
            if own is not None:
                inverse_sum[own, g] = inverse

        face_row(voids_near, near + 1, store)

    @pl.loop(0, ROWS, step=2)
    def _(start):
        for row in (start, start + 1):
            momentum_row(
                row + 1,
                lambda g, row=row: drag[row, g],
                lambda g, row=row: [force[k, row, g] for k in range(3)],
                row,
            )

    for message, side in ((first, Side(True)), (second, Side(False))):
        momentum_row(
            side.at(ROWS + 1, 0), lambda g, m=message: m[2, g], lambda g, m=message: [m[3, g]]
        )


def outer_kernel(voids_near, first, second, near_weights, weights, wide):
    for message, side in ((first, Side(True)), (second, Side(False))):
        at = side.at(2 * ROWS + 2, 0)
        for n in range(ROWS - 2):
            wide[at + n] = message[n] * side.there

    @pl.loop(0, ROWS + 4)
    def _(row):
        wide[row + ROWS - 2] = voids_near[row]

    @pl.loop(0, ROWS + 2)
    def _(row):
        weights[row + ROWS - 2] = near_weights[row]

    def outer_row(row):
        def store(g, scaled, void, total, inverse):
            for n in range(6):
                weights[row - 1, n, g] = scaled[n]

        face_row(wide, row, store)

    @pl.loop(1, ROWS - 1, step=2)
    def _(start):
        for row in (start, start + 1, start + 2 * ROWS, start + 2 * ROWS + 1):
            outer_row(row)


def edge_kernel(velocity, first, second):
    even = lax.rem(lax.axis_index("gy"), 2) == 0
    first_row = jnp.where(even, ROWS - 2, 0)
    for message, pair, single in (
        (first, first_row, jnp.where(even, ROWS - 1, 0)),
        (second, ROWS - 2 - first_row, jnp.where(even, 0, ROWS - 1)),
    ):
        for g in range(GROUPS):
            message[0, g] = velocity[g, 0, pair]
            message[1, g] = velocity[g, 0, pair + 1]
            message[2, g] = velocity[g, 1, single]
            message[3, g] = velocity[g, 2, single]


def momentum_kernel(
    velocity, first, second, weights, inverse_sum, centre, spread, given, voids_near, predicted, source, wide, flux
):
    for message, side in ((first, Side(True)), (second, Side(False))):
        pair = side.at(ROWS + 2, 0)
        single = side.at(ROWS + 2, 1)
        for g in range(GROUPS):
            wide[0, pair, g] = message[0, g] * side.there
            wide[0, pair + 1, g] = message[1, g] * side.there
            wide[1, single, g] = message[2, g] * side.there
            wide[2, single, g] = message[3, g] * side.there

    @pl.loop(0, ROWS, step=2)
    def _(start):
        for row in (start, start + 1):
            for g in range(GROUPS):
                for k in range(3):
                    wide[k, row + 2, g] = velocity[g, k, row]

    planes = plane_ids()

    def predict(k, near):
        tiles = [wide[k, near + 1, g] for g in range(GROUPS)]
        ups, downs = column_neighbours(tiles)
        for g in range(GROUPS):
            around = weighted_sum(
                weights, near, g, tiles[g], ups[g], downs[g], wide[k, near + 2, g], wide[k, near, g]
            )
            yield centre[near, g] * tiles[g] + spread[near, g] * around + given[k, near, g]

    @pl.loop(0, ROWS + 2, step=5)
    def _(start):
        for near in range(5):
            for g, value in enumerate(predict(0, start + near)):
                flux[0, start + near, g] = value
                flux[1, start + near, g] = voids_near[start + near + 1, g] * value

    @pl.loop(0, ROWS, step=4)
    def _(start):
        for row in range(4):
            row = start + row
            near = row + 1
            second_flux = []
            for g, value in enumerate(predict(1, near)):
                predicted[1, row, g] = value
                second_flux.append(voids_near[near + 1, g] * value)
            ups, downs = column_neighbours(second_flux)
            for g, value in enumerate(predict(2, near)):
                predicted[2, row, g] = value
                predicted[0, row, g] = flux[0, near, g]
                third_flux = voids_near[near + 1, g] * value
                change = flux[1, near + 1, g] - flux[1, near - 1, g]
                change = change + (no_column_up(g, ups[g]) - no_column_down(g, downs[g]))
                change = change + (
                    jnp.where(planes == PLANES - 1, 0.0, plane_up(third_flux))
                    - jnp.where(planes == 0, 0.0, plane_down(third_flux))
                )
                source[row, g] = change * inverse_sum[row, g]


def sweep_kernel(source, first, second, weights, pressure, near_pressure, source_wide, one, other):
    sides = Side(True).at(2 * ROWS, 0), Side(False).at(2 * ROWS, 0)
    there = Side(True).there, Side(False).there

    @pl.loop(0, ROWS, step=2)
    def _(start):
        for row in (start, start + 1):
            for at, value in (
                (sides[0] + row, first[row] * there[0]),
                (sides[1] + row, second[row] * there[1]),
                (ROWS + row, source[row]),
            ):
                source_wide[at] = value
                one[at] = -value

    def sweep_row(row, now, store):
        tiles = [now[row, g] for g in range(GROUPS)]
        ups, downs = column_neighbours(tiles)
        for g in range(GROUPS):
            around = weighted_sum(weights, row - 1, g, tiles[g], ups[g], downs[g], now[row + 1, g], now[row - 1, g])
            store(row, g, around - source_wide[row, g])

    now, later = one, other
    for sweep in range(1, SWEEPS - 1):
        half = (WIDE - 2 * sweep) // 2

        def half_sweep(start, now=now, later=later, half=half):
            def store(row, g, value):
                later[row, g] = value

            for row in range(half):
                sweep_row(start + row, now, store)

        pl.loop(sweep, WIDE - sweep, step=half)(half_sweep)
        now, later = later, now

    def keep(row, g, value):
        near_pressure[row - (ROWS - 1), g] = value

    @pl.loop(0, ROWS, step=4)
    def _(start):
        def store(row, g, value):
            keep(row, g, value)
            pressure[g, row - ROWS] = value

        for row in range(4):
            sweep_row(ROWS + start + row, now, store)

    for row in (ROWS - 1, 2 * ROWS):
        sweep_row(row, now, keep)


def correct_kernel(near_pressure, predicted, velocity, slopes):
    planes = plane_ids()
    held = [[[None] * ROWS for _ in range(GROUPS)] for _ in range(3)]
    for row in range(ROWS):
        tiles = [near_pressure[row + 1, g] for g in range(GROUPS)]
        ups, downs = column_neighbours(tiles)
        for g in range(GROUPS):
            tile = tiles[g]
            held[0][g][row] = 0.5 * (near_pressure[row + 2, g] - near_pressure[row, g])
            held[1][g][row] = 0.5 * (no_column_up(g, ups[g]) - no_column_down(g, downs[g]))
            held[2][g][row] = 0.5 * (
                jnp.where(planes == PLANES - 1, 0.0, plane_up(tile)) - jnp.where(planes == 0, 0.0, plane_down(tile))
            )
    for g in range(GROUPS):
        columns = pl.ds(g * LANES, LANES)
        for k in range(3):
            slope = jnp.stack(held[k][g])
            slopes[k, :, :, columns] = jnp.swapaxes(slope, 0, 1)
            velocity[k, :, :, columns] = jnp.swapaxes(predicted[k, :, g] - time_step * slope, 0, 1)


def call(kernel, args, outs, scratch=(), vmem=16, to=pltpu.VMEM, flops=0):
    spec = pl.BlockSpec(memory_space=pltpu.VMEM)
    shapes = [jax.ShapeDtypeStruct(shape, f32) for shape in outs]
    moved = sum(arg.size for arg in args) * 4 + sum(shape.size for shape in shapes) * 4
    return pl.pallas_call(
        kernel,
        out_shape=shapes,
        in_specs=[spec] * len(args),
        out_specs=[pl.BlockSpec(memory_space=to)] * len(outs),
        scratch_shapes=[pltpu.VMEM(shape, f32) if isinstance(shape, tuple) else shape for shape in scratch],
        cost_estimate=pl.CostEstimate(flops=flops, bytes_accessed=moved, transcendentals=0),
        compiler_params=pltpu.CompilerParams(vmem_limit_bytes=vmem * 1024 * 1024),
        name=kernel.__name__,
    )(*args)


def swap(first, second):
    devices = lax.axis_size("gx") * lax.axis_size("gy")
    inner = [(d, d ^ 1) for d in range(devices)]
    outer = [(d, (((d + 1) % devices) ^ 1) - 1) for d in range(devices)]
    outer = [(a, b % devices) for a, b in outer]
    return lax.ppermute(first, AXES, inner), lax.ppermute(second, AXES, outer)


def shards(particle_count, drag_coeff, particle_velocity, fluid_velocity):
    along, across = lax.axis_size("gy"), lax.axis_size("gx")
    field = (GROUPS, PLANES, LANES)
    own = (ROWS,) + field
    near = (ROWS + 2,) + field

    voids, drag, force, first, second, first_far, second_far = call(
        particle_kernel,
        (particle_count, drag_coeff, particle_velocity),
        [own, own, (3,) + own, (4,) + field, (4,) + field, (ROWS - 2,) + field, (ROWS - 2,) + field],
    )
    (blocks,) = call(
        block_kernel,
        (fluid_velocity,),
        [(along, across // along, 3, ROWS, PLANES, LANES)],
        [
            (along, across // along, 3, ROWS, PLANES, LANES),
            pltpu.SemaphoreType.DMA((3, across // along)),
        ],
        to=pl.ANY,
    )
    blocks = lax.all_to_all(blocks, "gy", split_axis=0, concat_axis=0, tiled=True)
    blocks, first, second = lax.optimization_barrier((blocks, first, second))
    first, second = swap(first, second)
    blocks = blocks.reshape(across, 3, ROWS, PLANES, LANES)
    slab = lax.all_to_all(blocks, "gx", split_axis=0, concat_axis=0, tiled=True)
    near_weights, inverse_sum, centre, spread, given, voids_near = call(
        coefficient_kernel,
        (voids, drag, force, first, second),
        [(ROWS + 2, 6) + field, own, near, near, (3,) + near, (ROWS + 4,) + field],
        flops=COVER,
    )

    edges = call(edge_kernel, (slab,), [(4,) + field] * 2)
    *edges, first_far, second_far = lax.optimization_barrier((*edges, first_far, second_far))
    first, second = swap(*edges)
    first_far, second_far = swap(first_far, second_far)
    predicted, source = call(
        momentum_kernel,
        (slab, first, second, near_weights, inverse_sum, centre, spread, given, voids_near),
        [(3,) + own, own],
        [(3, ROWS + 4) + field, (2,) + near],
    )
    (weights,) = call(
        outer_kernel,
        (voids_near, first_far, second_far, near_weights),
        [(WIDE - 2, 6) + field],
        [(WIDE,) + field],
        flops=COVER,
    )
    first, second = swap(source, source)
    pressure, near_pressure = call(
        sweep_kernel,
        (source, first, second, weights),
        [(GROUPS, ROWS, PLANES, LANES), near],
        [(WIDE,) + field] * 3,
    )

    velocity, slopes = call(
        correct_kernel, (near_pressure, predicted), [(3, PLANES, ROWS, GROUPS * LANES)] * 2
    )

    pressure = lax.all_to_all(pressure, "gx", split_axis=0, concat_axis=0, tiled=True)
    pressure = lax.all_to_all(pressure, "gy", split_axis=0, concat_axis=0, tiled=True)
    pressure = pressure.reshape(along, across // along, ROWS, PLANES, LANES)
    pressure = pressure.transpose(3, 1, 0, 2, 4).reshape(PLANES, across * ROWS, LANES)
    return (pressure, velocity, slopes)


def solution(mesh):
    placed = (
        P(None, ("gx", "gy"), None),
        P(None, ("gx", "gy"), None),
        P(None, None, ("gx", "gy"), None),
        P(None, None, "gy", "gx"),
    )
    return jax.shard_map(
        shards,
        mesh=mesh,
        in_specs=placed,
        out_specs=(
            P(None, "gy", "gx"),
            P(None, None, ("gx", "gy"), None),
            P(None, None, ("gx", "gy"), None),
        ),
        check_vma=False,
    )
```

```python
import jax
import jax.numpy as jnp
from jax import lax
from jax.experimental import pallas as pl
from jax.experimental.pallas import tpu as pltpu
from jax.sharding import PartitionSpec as P

SWEEPS = 8

particle_volume = 0.05
time_step = 0.5
viscosity = 0.1

ROWS = 8
PLANES = 8
GROUPS = 16
LANES = 128
TILE = (PLANES, LANES)
WIDE = 3 * ROWS
HALF = ROWS // 2
COVER = 6_000_000_000
AXES = ("gx", "gy")
f32 = jnp.float32


def place():
    return lax.axis_index("gx") * lax.axis_size("gy") + lax.axis_index("gy")


def lane_ids():
    return lax.broadcasted_iota(jnp.int32, TILE, 1)


def plane_ids():
    return lax.broadcasted_iota(jnp.int32, TILE, 0)


def plane_up(tile):
    return pltpu.roll(tile, PLANES - 1, 0)


def plane_down(tile):
    return pltpu.roll(tile, 1, 0)


def column_neighbours(tiles):
    lanes = lane_ids()
    last, first = lanes == LANES - 1, lanes == 0
    ahead = [pltpu.roll(tile, LANES - 1, 1) for tile in tiles]
    behind = [pltpu.roll(tile, 1, 1) for tile in tiles]
    n = len(tiles)
    up = [jnp.where(last, ahead[g + 1], ahead[g]) if g < n - 1 else ahead[g] for g in range(n)]
    down = [jnp.where(first, behind[g - 1], behind[g]) if g > 0 else behind[g] for g in range(n)]
    return up, down


def no_column_up(g, tile):
    return jnp.where(lane_ids() == LANES - 1, 0.0, tile) if g == GROUPS - 1 else tile


def no_column_down(g, tile):
    return jnp.where(lane_ids() == 0, 0.0, tile) if g == 0 else tile


def weighted_sum(weights, row, g, tile, up, down, row_up, row_down):
    total = weights[row, 0, g] * plane_up(tile) + weights[row, 1, g] * plane_down(tile)
    total = total + (weights[row, 2, g] * row_up + weights[row, 3, g] * row_down)
    return total + (weights[row, 4, g] * up + weights[row, 5, g] * down)


def block_kernel(velocity, blocks, turned, left):
    along, groups = blocks.shape[:2]
    copies = []
    for k in range(3):
        for part in range(groups):
            for chunk in range(along):
                rows = velocity[k, :, pl.ds((part * along + chunk) * ROWS, ROWS), :]
                turned[chunk, part, k] = jnp.swapaxes(rows, 0, 1)
            copies.append(pltpu.make_async_copy(turned.at[:, part, k], blocks.at[:, part, k], left.at[k, part]))
            copies[-1].start()
    for copy in copies:
        copy.wait()


def particle_kernel(count, drag, velocity, voids, drag_out, force, first_near, second_near, first_far, second_far):
    even = lax.rem(lax.axis_index("gy"), 2) == 0
    for g in range(GROUPS):
        columns = pl.ds(g * LANES, LANES)
        voids[:, g] = jnp.swapaxes(1.0 - count[:, :, columns].astype(f32) * particle_volume, 0, 1)
        drags = drag[:, :, columns]
        drag_out[:, g] = jnp.swapaxes(drags, 0, 1)
        for k in range(3):
            force[k, :, g] = jnp.swapaxes(time_step * drags * velocity[k, :, :, columns], 0, 1)
    for near, far, last in ((first_near, first_far, even), (second_near, second_far, jnp.logical_not(even))):
        pair = jnp.where(last, ROWS - 2, 0)
        single = jnp.where(last, ROWS - 1, 0)
        rest = jnp.where(last, 0, 2)
        near[0:2] = voids[pl.ds(pair, 2)]
        near[2] = drag_out[single]
        near[3] = force[0, single]
        far[...] = voids[pl.ds(rest, ROWS - 2)]


class Side:
    def __init__(self, first):
        even = lax.rem(lax.axis_index("gy"), 2) == 0
        self.high = even if first else jnp.logical_not(even)
        devices = lax.axis_size("gx") * lax.axis_size("gy")
        low_there = (place() > 0).astype(f32)
        high_there = (place() < devices - 1).astype(f32)
        self.there = jnp.where(self.high, high_there, low_there)

    def at(self, high, low):
        return jnp.where(self.high, high, low)


def face_row(voids, row, store):
    planes = plane_ids()
    tiles = [voids[row, g] for g in range(GROUPS)]
    ups, downs = column_neighbours(tiles)
    for g in range(GROUPS):
        tile = tiles[g]
        near = [
            jnp.where(planes == PLANES - 1, 0.0, plane_up(tile)),
            jnp.where(planes == 0, 0.0, plane_down(tile)),
            voids[row + 1, g],
            voids[row - 1, g],
            no_column_up(g, ups[g]),
            no_column_down(g, downs[g]),
        ]
        faces = [0.5 * (tile + other) for other in near]
        total = faces[0]
        for face in faces[1:]:
            total = total + face
        inverse = jnp.where(tile > 0.0, 1.0 / total, 0.0)
        scaled = [face * inverse for face in faces]
        scaled[0] = jnp.where(planes == PLANES - 1, 0.0, scaled[0])
        scaled[1] = jnp.where(planes == 0, 0.0, scaled[1])
        scaled[4] = no_column_up(g, scaled[4])
        scaled[5] = no_column_down(g, scaled[5])
        store(g, scaled, tile, total, inverse)


def coefficient_kernel(voids, drag, force, first, second, weights, inverse_sum, centre, spread, given, voids_near):
    for message, side in ((first, Side(True)), (second, Side(False))):
        at = side.at(ROWS + 2, 0)
        for n in range(2):
            voids_near[at + n] = message[n] * side.there

    @pl.loop(0, ROWS)
    def _(row):
        voids_near[row + 2] = voids[row]

    def momentum_row(near, drag_at, force_at, own=None):
        def store(g, scaled, void, total, inverse):
            for n in range(6):
                weights[near, n, g] = scaled[n]
            scale = 1.0 / (void + time_step * drag_at(g))
            centre[near, g] = (void - time_step * viscosity * total) * scale
            spread[near, g] = (time_step * viscosity * total) * scale
            for k, value in enumerate(force_at(g)):
                given[k, near, g] = value * scale
            if own is not None:
                inverse_sum[own, g] = inverse

        face_row(voids_near, near + 1, store)

    @pl.loop(0, ROWS, step=2)
    def _(start):
        for row in (start, start + 1):
            momentum_row(
                row + 1,
                lambda g, row=row: drag[row, g],
                lambda g, row=row: [force[k, row, g] for k in range(3)],
                row,
            )

    for message, side in ((first, Side(True)), (second, Side(False))):
        momentum_row(
            side.at(ROWS + 1, 0), lambda g, m=message: m[2, g], lambda g, m=message: [m[3, g]]
        )


def outer_kernel(voids_near, first, second, near_weights, weights, wide):
    for message, side in ((first, Side(True)), (second, Side(False))):
        at = side.at(2 * ROWS + 2, 0)
        for n in range(ROWS - 2):
            wide[at + n] = message[n] * side.there

    @pl.loop(0, ROWS + 4)
    def _(row):
        wide[row + ROWS - 2] = voids_near[row]

    @pl.loop(0, ROWS + 2)
    def _(row):
        weights[row + ROWS - 2] = near_weights[row]

    def outer_row(row):
        def store(g, scaled, void, total, inverse):
            for n in range(6):
                weights[row - 1, n, g] = scaled[n]

        face_row(wide, row, store)

    @pl.loop(1, ROWS - 1, step=2)
    def _(start):
        for row in (start, start + 1, start + 2 * ROWS, start + 2 * ROWS + 1):
            outer_row(row)


def edge_kernel(velocity, first, second):
    even = lax.rem(lax.axis_index("gy"), 2) == 0
    first_row = jnp.where(even, ROWS - 2, 0)
    for message, pair, single in (
        (first, first_row, jnp.where(even, ROWS - 1, 0)),
        (second, ROWS - 2 - first_row, jnp.where(even, 0, ROWS - 1)),
    ):
        for g in range(GROUPS):
            message[0, g] = velocity[g, 0, pair]
            message[1, g] = velocity[g, 0, pair + 1]
            message[2, g] = velocity[g, 1, single]
            message[3, g] = velocity[g, 2, single]


def momentum_kernel(
    velocity, first, second, weights, inverse_sum, centre, spread, given, voids_near, predicted, source, first_half, second_half, wide, flux
):
    for message, side in ((first, Side(True)), (second, Side(False))):
        pair = side.at(ROWS + 2, 0)
        single = side.at(ROWS + 2, 1)
        for g in range(GROUPS):
            wide[0, pair, g] = message[0, g] * side.there
            wide[0, pair + 1, g] = message[1, g] * side.there
            wide[1, single, g] = message[2, g] * side.there
            wide[2, single, g] = message[3, g] * side.there

    @pl.loop(0, ROWS, step=2)
    def _(start):
        for row in (start, start + 1):
            for g in range(GROUPS):
                for k in range(3):
                    wide[k, row + 2, g] = velocity[g, k, row]

    planes = plane_ids()

    def predict(k, near):
        tiles = [wide[k, near + 1, g] for g in range(GROUPS)]
        ups, downs = column_neighbours(tiles)
        for g in range(GROUPS):
            around = weighted_sum(
                weights, near, g, tiles[g], ups[g], downs[g], wide[k, near + 2, g], wide[k, near, g]
            )
            yield centre[near, g] * tiles[g] + spread[near, g] * around + given[k, near, g]

    @pl.loop(0, ROWS + 2, step=5)
    def _(start):
        for near in range(5):
            for g, value in enumerate(predict(0, start + near)):
                flux[0, start + near, g] = value
                flux[1, start + near, g] = voids_near[start + near + 1, g] * value

    @pl.loop(0, ROWS, step=4)
    def _(start):
        for row in range(4):
            row = start + row
            near = row + 1
            second_flux = []
            for g, value in enumerate(predict(1, near)):
                predicted[1, row, g] = value
                second_flux.append(voids_near[near + 1, g] * value)
            ups, downs = column_neighbours(second_flux)
            for g, value in enumerate(predict(2, near)):
                predicted[2, row, g] = value
                predicted[0, row, g] = flux[0, near, g]
                third_flux = voids_near[near + 1, g] * value
                change = flux[1, near + 1, g] - flux[1, near - 1, g]
                change = change + (no_column_up(g, ups[g]) - no_column_down(g, downs[g]))
                change = change + (
                    jnp.where(planes == PLANES - 1, 0.0, plane_up(third_flux))
                    - jnp.where(planes == 0, 0.0, plane_down(third_flux))
                )
                source[row, g] = change * inverse_sum[row, g]

    upper = Side(True).at(HALF, 0)
    first_half[...] = source[pl.ds(upper, HALF)]
    second_half[...] = source[pl.ds(HALF - upper, HALF)]


def sweep_row(weights, at, source, now, row, store):
    tiles = [now[row, g] for g in range(GROUPS)]
    ups, downs = column_neighbours(tiles)
    for g in range(GROUPS):
        around = weighted_sum(weights, at, g, tiles[g], ups[g], downs[g], now[row + 1, g], now[row - 1, g])
        store(g, around - source[g])


def inner_kernel(source, first, second, weights, near_source, edges, middle, one, other):
    for message, side in ((first, Side(True)), (second, Side(False))):
        at = side.at(HALF + ROWS, 0)
        for row in range(HALF):
            near_source[at + row] = message[row] * side.there
    near_source[HALF : HALF + ROWS] = source[...]

    @pl.loop(0, 2 * ROWS, step=2)
    def _(start):
        for row in (start, start + 1):
            one[row] = -near_source[row]

    now, later = one, other
    for sweep in range(1, SWEEPS):
        edges[sweep - 1, 0:2] = now[sweep - 1 : sweep + 1]
        edges[sweep - 1, 2:4] = now[2 * ROWS - 1 - sweep : 2 * ROWS + 1 - sweep]
        half = ROWS - sweep

        def half_sweep(start, now=now, later=later, half=half):
            for n in range(half):
                row = start + n

                def store(g, value, row=row):
                    later[row, g] = value

                sweep_row(weights, row + HALF - 1, near_source.at[row], now, row, store)

        pl.loop(sweep, 2 * ROWS - sweep, step=half)(half_sweep)
        now, later = later, now
    middle[...] = now[ROWS - 1 : ROWS + 1]


def rim_kernel(near_source, first, second, edges, middle, weights, pressure, near_pressure, source_wide, low, high):
    for message, side in ((first, Side(True)), (second, Side(False))):
        at = side.at(HALF + 2 * ROWS, 0)
        for row in range(HALF):
            source_wide[at + row] = message[row] * side.there

    @pl.loop(0, 2 * ROWS, step=2)
    def _(start):
        for row in (start, start + 1):
            source_wide[HALF + row] = near_source[row]

    for row in range(HALF):
        low[0, row] = -source_wide[row]
        high[0, row + 2] = -source_wide[WIDE - HALF + row]

    @pl.loop(1, SWEEPS)
    def _(sweep):
        now = lax.rem(sweep + 1, 2)
        later = 1 - now
        for n in range(2):
            low[now, HALF + n] = edges[sweep - 1, n]
            high[now, n] = edges[sweep - 1, 2 + n]
        for n in range(HALF):

            def store_low(g, value, n=n):
                low[later, n, g] = value

            def store_high(g, value, n=n):
                high[later, n + 2, g] = value

            row = sweep + n
            sweep_row(weights, row - 1, source_wide.at[row], low.at[now], n + 1, store_low)
            row = WIDE - HALF - sweep + n
            sweep_row(weights, row - 1, source_wide.at[row], high.at[now], n + 1, store_high)

    last = (SWEEPS - 1) % 2
    rows = [low.at[last, n] for n in range(HALF)] + [middle.at[n] for n in range(2)]
    rows = rows + [high.at[last, n + 2] for n in range(HALF)]
    for n, row in enumerate(rows):
        near_pressure[n] = row[...]
        if 0 < n <= ROWS:
            pressure[:, n - 1] = row[...]


def correct_kernel(near_pressure, predicted, velocity, slopes):
    planes = plane_ids()
    held = [[[None] * ROWS for _ in range(GROUPS)] for _ in range(3)]
    for row in range(ROWS):
        tiles = [near_pressure[row + 1, g] for g in range(GROUPS)]
        ups, downs = column_neighbours(tiles)
        for g in range(GROUPS):
            tile = tiles[g]
            held[0][g][row] = 0.5 * (near_pressure[row + 2, g] - near_pressure[row, g])
            held[1][g][row] = 0.5 * (no_column_up(g, ups[g]) - no_column_down(g, downs[g]))
            held[2][g][row] = 0.5 * (
                jnp.where(planes == PLANES - 1, 0.0, plane_up(tile)) - jnp.where(planes == 0, 0.0, plane_down(tile))
            )
    for g in range(GROUPS):
        columns = pl.ds(g * LANES, LANES)
        for k in range(3):
            slope = jnp.stack(held[k][g])
            slopes[k, :, :, columns] = jnp.swapaxes(slope, 0, 1)
            velocity[k, :, :, columns] = jnp.swapaxes(predicted[k, :, g] - time_step * slope, 0, 1)


def call(kernel, args, outs, scratch=(), vmem=16, to=pltpu.VMEM, flops=0):
    spec = pl.BlockSpec(memory_space=pltpu.VMEM)
    shapes = [jax.ShapeDtypeStruct(shape, f32) for shape in outs]
    moved = sum(arg.size for arg in args) * 4 + sum(shape.size for shape in shapes) * 4
    return pl.pallas_call(
        kernel,
        out_shape=shapes,
        in_specs=[spec] * len(args),
        out_specs=[pl.BlockSpec(memory_space=to)] * len(outs),
        scratch_shapes=[pltpu.VMEM(shape, f32) if isinstance(shape, tuple) else shape for shape in scratch],
        cost_estimate=pl.CostEstimate(flops=flops, bytes_accessed=moved, transcendentals=0),
        compiler_params=pltpu.CompilerParams(vmem_limit_bytes=vmem * 1024 * 1024),
        name=kernel.__name__,
    )(*args)


def swap(first, second):
    devices = lax.axis_size("gx") * lax.axis_size("gy")
    inner = [(d, d ^ 1) for d in range(devices)]
    outer = [(d, ((((d + 1) % devices) ^ 1) - 1) % devices) for d in range(devices)]
    return lax.ppermute(first, AXES, inner), lax.ppermute(second, AXES, outer)


def shards(particle_count, drag_coeff, particle_velocity, fluid_velocity):
    along, across = lax.axis_size("gy"), lax.axis_size("gx")
    field = (GROUPS, PLANES, LANES)
    own = (ROWS,) + field
    near = (ROWS + 2,) + field

    voids, drag, force, first, second, first_far, second_far = call(
        particle_kernel,
        (particle_count, drag_coeff, particle_velocity),
        [own, own, (3,) + own, (4,) + field, (4,) + field, (ROWS - 2,) + field, (ROWS - 2,) + field],
    )
    (blocks,) = call(
        block_kernel,
        (fluid_velocity,),
        [(along, across // along, 3, ROWS, PLANES, LANES)],
        [
            (along, across // along, 3, ROWS, PLANES, LANES),
            pltpu.SemaphoreType.DMA((3, across // along)),
        ],
        to=pl.ANY,
    )
    blocks = lax.all_to_all(blocks, "gy", split_axis=0, concat_axis=0, tiled=True)
    blocks, first, second = lax.optimization_barrier((blocks, first, second))
    first, second = swap(first, second)
    blocks = blocks.reshape(across, 3, ROWS, PLANES, LANES)
    slab = lax.all_to_all(blocks, "gx", split_axis=0, concat_axis=0, tiled=True)
    near_weights, inverse_sum, centre, spread, given, voids_near = call(
        coefficient_kernel,
        (voids, drag, force, first, second),
        [(ROWS + 2, 6) + field, own, near, near, (3,) + near, (ROWS + 4,) + field],
        flops=COVER,
    )

    edges = call(edge_kernel, (slab,), [(4,) + field] * 2)
    *edges, first_far, second_far = lax.optimization_barrier((*edges, first_far, second_far))
    first, second = swap(*edges)
    first_far, second_far = swap(first_far, second_far)
    predicted, source, first_half, second_half = call(
        momentum_kernel,
        (slab, first, second, near_weights, inverse_sum, centre, spread, given, voids_near),
        [(3,) + own, own, (HALF,) + field, (HALF,) + field],
        [(3, ROWS + 4) + field, (2,) + near],
    )
    (weights,) = call(
        outer_kernel,
        (voids_near, first_far, second_far, near_weights),
        [(WIDE - 2, 6) + field],
        [(WIDE,) + field],
        flops=COVER,
    )
    first, second = swap(first_half, second_half)
    second_half, first_half, weights = lax.optimization_barrier((second_half, first_half, weights))
    first_far, second_far = swap(second_half, first_half)
    near_source, edges, middle = call(
        inner_kernel,
        (source, first, second, weights),
        [(2 * ROWS,) + field, (SWEEPS - 1, 4) + field, (2,) + field],
        [(2 * ROWS,) + field] * 2,
        flops=COVER,
    )
    pressure, near_pressure = call(
        rim_kernel,
        (near_source, first_far, second_far, edges, middle, weights),
        [(GROUPS, ROWS, PLANES, LANES), near],
        [(WIDE,) + field, (2, HALF + 2) + field, (2, HALF + 2) + field],
    )

    velocity, slopes = call(
        correct_kernel, (near_pressure, predicted), [(3, PLANES, ROWS, GROUPS * LANES)] * 2
    )

    pressure = lax.all_to_all(pressure, "gx", split_axis=0, concat_axis=0, tiled=True)
    pressure = lax.all_to_all(pressure, "gy", split_axis=0, concat_axis=0, tiled=True)
    pressure = pressure.reshape(along, across // along, ROWS, PLANES, LANES)
    pressure = pressure.transpose(3, 1, 0, 2, 4).reshape(PLANES, across * ROWS, LANES)
    return (pressure, velocity, slopes)


def solution(mesh):
    placed = (
        P(None, ("gx", "gy"), None),
        P(None, ("gx", "gy"), None),
        P(None, None, ("gx", "gy"), None),
        P(None, None, "gy", "gx"),
    )
    return jax.shard_map(
        shards,
        mesh=mesh,
        in_specs=placed,
        out_specs=(
            P(None, "gy", "gx"),
            P(None, None, ("gx", "gy"), None),
            P(None, None, ("gx", "gy"), None),
        ),
        check_vma=False,
    )
```

```python
import jax
import jax.numpy as jnp
from jax import lax
from jax.experimental import pallas as pl
from jax.experimental.pallas import tpu as pltpu
from jax.sharding import PartitionSpec as P

SWEEPS = 8

particle_volume = 0.05
time_step = 0.5
viscosity = 0.1

ROWS = 8
PLANES = 8
GROUPS = 16
LANES = 128
TILE = (PLANES, LANES)
WIDE = 3 * ROWS
HALF = ROWS // 2
COVER = 6_000_000_000
AXES = ("gx", "gy")
f32 = jnp.float32


def place():
    return lax.axis_index("gx") * lax.axis_size("gy") + lax.axis_index("gy")


def lane_ids():
    return lax.broadcasted_iota(jnp.int32, TILE, 1)


def plane_ids():
    return lax.broadcasted_iota(jnp.int32, TILE, 0)


def plane_up(tile):
    return pltpu.roll(tile, PLANES - 1, 0)


def plane_down(tile):
    return pltpu.roll(tile, 1, 0)


def column_neighbours(tiles):
    lanes = lane_ids()
    last, first = lanes == LANES - 1, lanes == 0
    ahead = [pltpu.roll(tile, LANES - 1, 1) for tile in tiles]
    behind = [pltpu.roll(tile, 1, 1) for tile in tiles]
    n = len(tiles)
    up = [jnp.where(last, ahead[g + 1], ahead[g]) if g < n - 1 else ahead[g] for g in range(n)]
    down = [jnp.where(first, behind[g - 1], behind[g]) if g > 0 else behind[g] for g in range(n)]
    return up, down


def no_column_up(g, tile):
    return jnp.where(lane_ids() == LANES - 1, 0.0, tile) if g == GROUPS - 1 else tile


def no_column_down(g, tile):
    return jnp.where(lane_ids() == 0, 0.0, tile) if g == 0 else tile


def weighted_sum(weights, row, g, tile, up, down, row_up, row_down):
    total = weights[row, 0, g] * plane_up(tile) + weights[row, 1, g] * plane_down(tile)
    total = total + (weights[row, 2, g] * row_up + weights[row, 3, g] * row_down)
    return total + (weights[row, 4, g] * up + weights[row, 5, g] * down)


def block_kernel(velocity, blocks, turned, left):
    along, groups = blocks.shape[:2]
    copies = []
    for k in range(3):
        for part in range(groups):
            for chunk in range(along):
                rows = velocity[k, :, pl.ds((part * along + chunk) * ROWS, ROWS), :]
                turned[chunk, part, k] = jnp.swapaxes(rows, 0, 1)
            copies.append(pltpu.make_async_copy(turned.at[:, part, k], blocks.at[:, part, k], left.at[k, part]))
            copies[-1].start()
    for copy in copies:
        copy.wait()


def particle_kernel(count, drag, velocity, voids, drag_out, force, first_near, second_near, first_far, second_far):
    even = lax.rem(lax.axis_index("gy"), 2) == 0
    for g in range(GROUPS):
        columns = pl.ds(g * LANES, LANES)
        voids[:, g] = jnp.swapaxes(1.0 - count[:, :, columns].astype(f32) * particle_volume, 0, 1)
        drags = drag[:, :, columns]
        drag_out[:, g] = jnp.swapaxes(drags, 0, 1)
        for k in range(3):
            force[k, :, g] = jnp.swapaxes(time_step * drags * velocity[k, :, :, columns], 0, 1)
    for near, far, last in ((first_near, first_far, even), (second_near, second_far, jnp.logical_not(even))):
        pair = jnp.where(last, ROWS - 2, 0)
        single = jnp.where(last, ROWS - 1, 0)
        rest = jnp.where(last, 0, 2)
        near[0:2] = voids[pl.ds(pair, 2)]
        near[2] = drag_out[single]
        near[3] = force[0, single]
        far[...] = voids[pl.ds(rest, ROWS - 2)]


class Side:
    def __init__(self, first):
        even = lax.rem(lax.axis_index("gy"), 2) == 0
        self.high = even if first else jnp.logical_not(even)
        devices = lax.axis_size("gx") * lax.axis_size("gy")
        low_there = (place() > 0).astype(f32)
        high_there = (place() < devices - 1).astype(f32)
        self.there = jnp.where(self.high, high_there, low_there)

    def at(self, high, low):
        return jnp.where(self.high, high, low)


def face_row(voids, row, store):
    planes = plane_ids()
    tiles = [voids[row, g] for g in range(GROUPS)]
    ups, downs = column_neighbours(tiles)
    for g in range(GROUPS):
        tile = tiles[g]
        near = [
            jnp.where(planes == PLANES - 1, 0.0, plane_up(tile)),
            jnp.where(planes == 0, 0.0, plane_down(tile)),
            voids[row + 1, g],
            voids[row - 1, g],
            no_column_up(g, ups[g]),
            no_column_down(g, downs[g]),
        ]
        faces = [0.5 * (tile + other) for other in near]
        total = faces[0]
        for face in faces[1:]:
            total = total + face
        inverse = jnp.where(tile > 0.0, 1.0 / total, 0.0)
        scaled = [face * inverse for face in faces]
        scaled[0] = jnp.where(planes == PLANES - 1, 0.0, scaled[0])
        scaled[1] = jnp.where(planes == 0, 0.0, scaled[1])
        scaled[4] = no_column_up(g, scaled[4])
        scaled[5] = no_column_down(g, scaled[5])
        store(g, scaled, tile, total, inverse)


def coefficient_kernel(voids, drag, force, first, second, weights, inverse_sum, centre, spread, given, voids_near):
    for message, side in ((first, Side(True)), (second, Side(False))):
        at = side.at(ROWS + 2, 0)
        for n in range(2):
            voids_near[at + n] = message[n] * side.there

    @pl.loop(0, ROWS)
    def _(row):
        voids_near[row + 2] = voids[row]

    def momentum_row(near, drag_at, force_at, own=None):
        def store(g, scaled, void, total, inverse):
            for n in range(6):
                weights[near, n, g] = scaled[n]
            scale = 1.0 / (void + time_step * drag_at(g))
            centre[near, g] = (void - time_step * viscosity * total) * scale
            spread[near, g] = (time_step * viscosity * total) * scale
            for k, value in enumerate(force_at(g)):
                given[k, near, g] = value * scale
            if own is not None:
                inverse_sum[own, g] = inverse

        face_row(voids_near, near + 1, store)

    @pl.loop(0, ROWS, step=2)
    def _(start):
        for row in (start, start + 1):
            momentum_row(
                row + 1,
                lambda g, row=row: drag[row, g],
                lambda g, row=row: [force[k, row, g] for k in range(3)],
                row,
            )

    for message, side in ((first, Side(True)), (second, Side(False))):
        momentum_row(
            side.at(ROWS + 1, 0), lambda g, m=message: m[2, g], lambda g, m=message: [m[3, g]]
        )


def outer_kernel(voids_near, first, second, near_weights, weights, wide):
    for message, side in ((first, Side(True)), (second, Side(False))):
        at = side.at(2 * ROWS + 2, 0)
        for n in range(ROWS - 2):
            wide[at + n] = message[n] * side.there

    @pl.loop(0, ROWS + 4)
    def _(row):
        wide[row + ROWS - 2] = voids_near[row]

    @pl.loop(0, ROWS + 2)
    def _(row):
        weights[row + ROWS - 2] = near_weights[row]

    def outer_row(row):
        def store(g, scaled, void, total, inverse):
            for n in range(6):
                weights[row - 1, n, g] = scaled[n]

        face_row(wide, row, store)

    @pl.loop(1, ROWS - 1, step=2)
    def _(start):
        for row in (start, start + 1, start + 2 * ROWS, start + 2 * ROWS + 1):
            outer_row(row)


def edge_kernel(velocity, first, second):
    even = lax.rem(lax.axis_index("gy"), 2) == 0
    first_row = jnp.where(even, ROWS - 2, 0)
    for message, pair, single in (
        (first, first_row, jnp.where(even, ROWS - 1, 0)),
        (second, ROWS - 2 - first_row, jnp.where(even, 0, ROWS - 1)),
    ):
        for g in range(GROUPS):
            message[0, g] = velocity[g, 0, pair]
            message[1, g] = velocity[g, 0, pair + 1]
            message[2, g] = velocity[g, 1, single]
            message[3, g] = velocity[g, 2, single]


def momentum_kernel(
    velocity, first, second, weights, inverse_sum, centre, spread, given, voids_near, predicted, source, first_half, second_half, wide, flux
):
    for message, side in ((first, Side(True)), (second, Side(False))):
        pair = side.at(ROWS + 2, 0)
        single = side.at(ROWS + 2, 1)
        for g in range(GROUPS):
            wide[0, pair, g] = message[0, g] * side.there
            wide[0, pair + 1, g] = message[1, g] * side.there
            wide[1, single, g] = message[2, g] * side.there
            wide[2, single, g] = message[3, g] * side.there

    @pl.loop(0, ROWS, step=2)
    def _(start):
        for row in (start, start + 1):
            for g in range(GROUPS):
                for k in range(3):
                    wide[k, row + 2, g] = velocity[g, k, row]

    planes = plane_ids()

    def predict(k, near):
        tiles = [wide[k, near + 1, g] for g in range(GROUPS)]
        ups, downs = column_neighbours(tiles)
        for g in range(GROUPS):
            around = weighted_sum(
                weights, near, g, tiles[g], ups[g], downs[g], wide[k, near + 2, g], wide[k, near, g]
            )
            yield centre[near, g] * tiles[g] + spread[near, g] * around + given[k, near, g]

    @pl.loop(0, ROWS + 2, step=5)
    def _(start):
        for near in range(5):
            for g, value in enumerate(predict(0, start + near)):
                flux[0, start + near, g] = value
                flux[1, start + near, g] = voids_near[start + near + 1, g] * value

    @pl.loop(0, ROWS, step=4)
    def _(start):
        for row in range(4):
            row = start + row
            near = row + 1
            second_flux = []
            for g, value in enumerate(predict(1, near)):
                predicted[1, row, g] = value
                second_flux.append(voids_near[near + 1, g] * value)
            ups, downs = column_neighbours(second_flux)
            for g, value in enumerate(predict(2, near)):
                predicted[2, row, g] = value
                predicted[0, row, g] = flux[0, near, g]
                third_flux = voids_near[near + 1, g] * value
                change = flux[1, near + 1, g] - flux[1, near - 1, g]
                change = change + (no_column_up(g, ups[g]) - no_column_down(g, downs[g]))
                change = change + (
                    jnp.where(planes == PLANES - 1, 0.0, plane_up(third_flux))
                    - jnp.where(planes == 0, 0.0, plane_down(third_flux))
                )
                source[row, g] = change * inverse_sum[row, g]

    upper = Side(True).at(HALF, 0)
    first_half[...] = source[pl.ds(upper, HALF)]
    second_half[...] = source[pl.ds(HALF - upper, HALF)]


def sweep_row(weights, at, source, now, row, store):
    tiles = [now[row, g] for g in range(GROUPS)]
    ups, downs = column_neighbours(tiles)
    for g in range(GROUPS):
        around = weighted_sum(weights, at, g, tiles[g], ups[g], downs[g], now[row + 1, g], now[row - 1, g])
        store(g, around - source[g])


def inner_kernel(source, first, second, weights, near_source, edges, middle, one, other):
    for message, side in ((first, Side(True)), (second, Side(False))):
        at = side.at(2 * ROWS, HALF)
        for row in range(HALF):
            near_source[at + row] = message[row] * side.there
    near_source[ROWS : 2 * ROWS] = source[...]

    @pl.loop(0, 2 * ROWS, step=2)
    def _(start):
        for row in (start, start + 1):
            one[row] = -near_source[row + HALF]

    now, later = one, other
    for sweep in range(1, SWEEPS):
        edges[sweep - 1, 0:2] = now[sweep - 1 : sweep + 1]
        edges[sweep - 1, 2:4] = now[2 * ROWS - 1 - sweep : 2 * ROWS + 1 - sweep]
        half = ROWS - sweep

        def half_sweep(start, now=now, later=later, half=half):
            for n in range(half):
                row = start + n

                def store(g, value, row=row):
                    later[row, g] = value

                sweep_row(weights, row + HALF - 1, near_source.at[row + HALF], now, row, store)

        pl.loop(sweep, 2 * ROWS - sweep, step=half)(half_sweep)
        now, later = later, now
    middle[...] = now[ROWS - 1 : ROWS + 1]


def rim_kernel(near_source, first, second, edges, middle, weights, source_wide, pressure, near_pressure, low, high):
    for message, side in ((first, Side(True)), (second, Side(False))):
        at = side.at(HALF + 2 * ROWS, 0)
        for row in range(HALF):
            source_wide[at + row] = message[row] * side.there

    for row in range(HALF):
        low[0, row] = -source_wide[row]
        high[0, row + 2] = -source_wide[WIDE - HALF + row]

    @pl.loop(1, SWEEPS)
    def _(sweep):
        now = lax.rem(sweep + 1, 2)
        later = 1 - now
        for n in range(2):
            low[now, HALF + n] = edges[sweep - 1, n]
            high[now, n] = edges[sweep - 1, 2 + n]
        for n in range(HALF):

            def store_low(g, value, n=n):
                low[later, n, g] = value

            def store_high(g, value, n=n):
                high[later, n + 2, g] = value

            row = sweep + n
            sweep_row(weights, row - 1, source_wide.at[row], low.at[now], n + 1, store_low)
            row = WIDE - HALF - sweep + n
            sweep_row(weights, row - 1, source_wide.at[row], high.at[now], n + 1, store_high)

    last = (SWEEPS - 1) % 2
    rows = [low.at[last, n] for n in range(HALF)] + [middle.at[n] for n in range(2)]
    rows = rows + [high.at[last, n + 2] for n in range(HALF)]
    for n, row in enumerate(rows):
        near_pressure[n] = row[...]
        if 0 < n <= ROWS:
            pressure[:, n - 1] = row[...]


def correct_kernel(near_pressure, predicted, velocity, slopes):
    planes = plane_ids()
    held = [[[None] * ROWS for _ in range(GROUPS)] for _ in range(3)]
    for row in range(ROWS):
        tiles = [near_pressure[row + 1, g] for g in range(GROUPS)]
        ups, downs = column_neighbours(tiles)
        for g in range(GROUPS):
            tile = tiles[g]
            held[0][g][row] = 0.5 * (near_pressure[row + 2, g] - near_pressure[row, g])
            held[1][g][row] = 0.5 * (no_column_up(g, ups[g]) - no_column_down(g, downs[g]))
            held[2][g][row] = 0.5 * (
                jnp.where(planes == PLANES - 1, 0.0, plane_up(tile)) - jnp.where(planes == 0, 0.0, plane_down(tile))
            )
    for g in range(GROUPS):
        columns = pl.ds(g * LANES, LANES)
        for k in range(3):
            slope = jnp.stack(held[k][g])
            slopes[k, :, :, columns] = jnp.swapaxes(slope, 0, 1)
            velocity[k, :, :, columns] = jnp.swapaxes(predicted[k, :, g] - time_step * slope, 0, 1)


def call(kernel, args, outs, scratch=(), vmem=16, to=pltpu.VMEM, flops=0, aliases={}):
    spec = pl.BlockSpec(memory_space=pltpu.VMEM)
    shapes = [jax.ShapeDtypeStruct(shape, f32) for shape in outs]
    moved = sum(arg.size for arg in args) * 4 + sum(shape.size for shape in shapes) * 4
    return pl.pallas_call(
        kernel,
        out_shape=shapes,
        in_specs=[spec] * len(args),
        out_specs=[pl.BlockSpec(memory_space=to)] * len(outs),
        scratch_shapes=[pltpu.VMEM(shape, f32) if isinstance(shape, tuple) else shape for shape in scratch],
        cost_estimate=pl.CostEstimate(flops=flops, bytes_accessed=moved, transcendentals=0),
        compiler_params=pltpu.CompilerParams(vmem_limit_bytes=vmem * 1024 * 1024),
        input_output_aliases=aliases,
        name=kernel.__name__,
    )(*args)


def swap(first, second):
    devices = lax.axis_size("gx") * lax.axis_size("gy")
    inner = [(d, d ^ 1) for d in range(devices)]
    outer = [(d, ((((d + 1) % devices) ^ 1) - 1) % devices) for d in range(devices)]
    return lax.ppermute(first, AXES, inner), lax.ppermute(second, AXES, outer)


def shards(particle_count, drag_coeff, particle_velocity, fluid_velocity):
    along, across = lax.axis_size("gy"), lax.axis_size("gx")
    field = (GROUPS, PLANES, LANES)
    own = (ROWS,) + field
    near = (ROWS + 2,) + field

    voids, drag, force, first, second, first_far, second_far = call(
        particle_kernel,
        (particle_count, drag_coeff, particle_velocity),
        [own, own, (3,) + own, (4,) + field, (4,) + field, (ROWS - 2,) + field, (ROWS - 2,) + field],
    )
    (blocks,) = call(
        block_kernel,
        (fluid_velocity,),
        [(along, across // along, 3, ROWS, PLANES, LANES)],
        [
            (along, across // along, 3, ROWS, PLANES, LANES),
            pltpu.SemaphoreType.DMA((3, across // along)),
        ],
        to=pl.ANY,
    )
    blocks = lax.all_to_all(blocks, "gy", split_axis=0, concat_axis=0, tiled=True)
    blocks, first, second = lax.optimization_barrier((blocks, first, second))
    first, second = swap(first, second)
    blocks = blocks.reshape(across, 3, ROWS, PLANES, LANES)
    slab = lax.all_to_all(blocks, "gx", split_axis=0, concat_axis=0, tiled=True)
    near_weights, inverse_sum, centre, spread, given, voids_near = call(
        coefficient_kernel,
        (voids, drag, force, first, second),
        [(ROWS + 2, 6) + field, own, near, near, (3,) + near, (ROWS + 4,) + field],
        flops=COVER,
    )

    edges = call(edge_kernel, (slab,), [(4,) + field] * 2)
    *edges, first_far, second_far = lax.optimization_barrier((*edges, first_far, second_far))
    first, second = swap(*edges)
    first_far, second_far = swap(first_far, second_far)
    predicted, source, first_half, second_half = call(
        momentum_kernel,
        (slab, first, second, near_weights, inverse_sum, centre, spread, given, voids_near),
        [(3,) + own, own, (HALF,) + field, (HALF,) + field],
        [(3, ROWS + 4) + field, (2,) + near],
    )
    (weights,) = call(
        outer_kernel,
        (voids_near, first_far, second_far, near_weights),
        [(WIDE - 2, 6) + field],
        [(WIDE,) + field],
        flops=COVER,
    )
    first, second = swap(first_half, second_half)
    second_half, first_half, weights = lax.optimization_barrier((second_half, first_half, weights))
    first_far, second_far = swap(second_half, first_half)
    near_source, edges, middle = call(
        inner_kernel,
        (source, first, second, weights),
        [(WIDE,) + field, (SWEEPS - 1, 4) + field, (2,) + field],
        [(2 * ROWS,) + field] * 2,
        flops=COVER,
    )
    _, pressure, near_pressure = call(
        rim_kernel,
        (near_source, first_far, second_far, edges, middle, weights),
        [(WIDE,) + field, (GROUPS, ROWS, PLANES, LANES), near],
        [(2, HALF + 2) + field, (2, HALF + 2) + field],
        aliases={0: 0},
    )

    velocity, slopes = call(
        correct_kernel, (near_pressure, predicted), [(3, PLANES, ROWS, GROUPS * LANES)] * 2
    )

    pressure = lax.all_to_all(pressure, "gx", split_axis=0, concat_axis=0, tiled=True)
    pressure = lax.all_to_all(pressure, "gy", split_axis=0, concat_axis=0, tiled=True)
    pressure = pressure.reshape(along, across // along, ROWS, PLANES, LANES)
    pressure = pressure.transpose(3, 1, 0, 2, 4).reshape(PLANES, across * ROWS, LANES)
    return (pressure, velocity, slopes)


def solution(mesh):
    placed = (
        P(None, ("gx", "gy"), None),
        P(None, ("gx", "gy"), None),
        P(None, None, ("gx", "gy"), None),
        P(None, None, "gy", "gx"),
    )
    return jax.shard_map(
        shards,
        mesh=mesh,
        in_specs=placed,
        out_specs=(
            P(None, "gy", "gx"),
            P(None, None, ("gx", "gy"), None),
            P(None, None, ("gx", "gy"), None),
        ),
        check_vma=False,
    )
```
